128 devices in a mesh: row: 8 (over y, core), col: 16 (over x, z).
Axes of the slice: x: 4, y: 4, z: 4, core: 2. Of those that a mesh axis runs over, the one named last changes fastest.
Arguments:
- atoms: bfloat16 [16384, 128], P(('row', 'col')), may hold values from -6 to 6
- pair: bfloat16 [128, 2048, 2048], P(None, 'row', 'col'), may hold values from -6 to 6
- token_atoms: int32 [2048], replicated, may hold values from 1 to 24, as said below
- attn_bias: float32 [512, 4, 32, 128], P(('row', 'col')), may hold values from -8 to 320
- w_attn: bfloat16 [128, 512], replicated, may hold values from -0.5 to 0.5
- w_attn_out: bfloat16 [128, 128], replicated, may hold values from -0.5 to 0.5
- w_single: bfloat16 [128, 384], replicated, may hold values from -0.5 to 0.5
- w_pair_left: bfloat16 [384, 128], replicated, may hold values from -0.3125 to 0.3125
- w_pair_right: bfloat16 [384, 128], replicated, may hold values from -0.3125 to 0.3125
- w_atom_back: bfloat16 [384, 128], replicated, may hold values from -0.3125 to 0.3125
- w_tri_in: bfloat16 [128, 512], replicated, may hold values from -0.5 to 0.5
- w_tri_gate: bfloat16 [128, 128], replicated, may hold values from -0.5 to 0.5
- w_tri_out: bfloat16 [128, 128], replicated, may hold values from -0.5 to 0.5
Outputs:
- atoms_out: bfloat16 [16384, 128], P(('row', 'col'))
- pair_out: bfloat16 [128, 2048, 2048], P(None, 'row', 'col')
The draws below stay inside these ranges and needn't reach their ends.
Inputs may be any that keep to these rules, and one draw needn't show every extreme that they name: `token_atoms`: entries sum to 16384; the last 1280 tokens hold one atom each; the largest is exactly 24.
All inputs are finite; a program needn't handle non-finite values.
Results may differ from the reference program's by a relative error of at most 0.006.
Values may be sent and summed in bfloat16 or wider, within the bound.
No kernel may reach another device: no remote copies, remote signals or barrier semaphores. Data moves between devices by JAX's collectives and lax.ppermute only.
A program may use at most 192 MiB of HBM per device.

```python
import math
import jax
import jax.numpy as jnp
from jax import lax

CA = 128
HEADS = 4
QBLOCK = 32
KWIN = 128
CS = 384
CP = 128
TOKENS = 2048
ATOMS = 16384
MOST_ATOMS = 24


def draw_token_atoms(key, part):
    key = jax.random.fold_in(key, 11)
    keys = jax.random.split(key, 2)
    singles = 5 * TOKENS // 8
    residues = TOKENS - singles
    residue_atoms = ATOMS - singles
    base_len = residue_atoms // residues
    surplus = residue_atoms % residues
    position = jnp.arange(residues, dtype=jnp.int32)
    lengths = base_len + (position < surplus).astype(jnp.int32)
    swing_most = max(0, min(base_len - 1, MOST_ATOMS - base_len - 2))
    swings = jax.random.randint(keys[0], (residues // 2,), -swing_most, swing_most + 1).astype(jnp.int32)
    paired = jnp.stack([swings, -swings], axis=1).reshape(residues)
    lengths = lengths + paired
    pair_total = lengths[0] + lengths[1]
    lengths = lengths.at[0].set(MOST_ATOMS).at[1].set(pair_total - MOST_ATOMS)
    lengths = jax.random.permutation(keys[1], lengths)
    return jnp.concatenate([lengths.astype(jnp.int32), jnp.ones((singles,), jnp.int32)])


def draw_attn_bias(key, part):
    key = jax.random.fold_in(key, 7)
    keys = jax.random.split(key, 1)
    shape = (ATOMS // QBLOCK, HEADS, QBLOCK, KWIN)
    return jnp.clip(jax.random.normal(keys[0], shape, jnp.float32), -6.0, 6.0)


def shard_levels(stream_key, shape, shards, smallest, largest):
    def one(axis_at, shards_of):
        steps = jax.random.uniform(jax.random.fold_in(jax.random.fold_in(stream_key, 6), axis_at), (shards_of,), jnp.float32, smallest / len(shards), largest / len(shards))
        return jnp.repeat(jnp.exp(steps), shape[axis_at] // shards_of).reshape((-1,) + (1,) * (len(shape) - axis_at - 1))

    level = one(*shards[0])
    for cut in shards[1:]:
        level = level * one(*cut)
    return level


def normal_values(own_key, dims, scale, reach, shards=(), kind=jnp.bfloat16):
    values = jax.random.normal(own_key, dims, jnp.float32) * scale
    if len(shards) > 0:
        values = shard_levels(own_key, dims, shards, -0.22, 0.18) * values
    return jnp.clip(values, min=-reach, max=reach).astype(kind)


def setup_inputs(seed: int = 0) -> dict:
    streams_of = jax.random.split(jax.random.key(seed), 14)
    atoms = normal_values(streams_of[0], (ATOMS, CA), 1.0, 6.0, ((0, 128),))
    pair = normal_values(streams_of[1], (CP, TOKENS, TOKENS), 1.0, 6.0, ((1, 8), (2, 16)))
    token_atoms = draw_token_atoms(jax.random.fold_in(streams_of[13], 71), 0)
    attn_bias = draw_attn_bias(jax.random.fold_in(streams_of[13], 71), 0)
    w_attn = normal_values(streams_of[4], (CA, 4 * CA), CA ** -0.5, 0.5)
    w_attn_out = normal_values(streams_of[5], (CA, CA), CA ** -0.5, 0.5)
    w_single = normal_values(streams_of[6], (CA, CS), CA ** -0.5, 0.5)
    w_pair_left = normal_values(streams_of[7], (CS, CP), CS ** -0.5, 0.3125)
    w_pair_right = normal_values(streams_of[8], (CS, CP), CS ** -0.5, 0.3125)
    w_atom_back = normal_values(streams_of[9], (CS, CA), CS ** -0.5, 0.3125)
    w_tri_in = normal_values(streams_of[10], (CP, 4 * CP), CP ** -0.5, 0.5)
    w_tri_gate = normal_values(streams_of[11], (CP, CP), CP ** -0.5, 0.5)
    w_tri_out = normal_values(streams_of[12], (CP, CP), CP ** -0.5, 0.5)
    return {"atoms": atoms, "pair": pair, "token_atoms": token_atoms, "attn_bias": attn_bias, "w_attn": w_attn, "w_attn_out": w_attn_out, "w_single": w_single, "w_pair_left": w_pair_left, "w_pair_right": w_pair_right, "w_atom_back": w_atom_back, "w_tri_in": w_tri_in, "w_tri_gate": w_tri_gate, "w_tri_out": w_tri_out}


epsilon = 1e-05

def layer_norm(values, along):
    average = lax.optimization_barrier(jnp.mean(values, axis=along, keepdims=True))
    centred = values - average
    variance = lax.optimization_barrier(jnp.mean(centred * centred, axis=along, keepdims=True))
    return centred * lax.rsqrt(variance + epsilon)

def reference(atoms, pair, token_atoms, attn_bias, w_attn, w_attn_out, w_single, w_pair_left, w_pair_right, w_atom_back, w_tri_in, w_tri_gate, w_tri_out):
    head_dim = CA // HEADS
    margin = (KWIN - QBLOCK) // 2
    blocks = ATOMS // QBLOCK
    normed = layer_norm(atoms.astype(jnp.float32), 1).astype(jnp.bfloat16)
    projected = jnp.dot(normed, w_attn, preferred_element_type=jnp.float32)
    queries = projected[:, :CA].astype(jnp.bfloat16)
    key_value = projected[:, CA:3 * CA].astype(jnp.bfloat16)
    gating = jax.nn.sigmoid(projected[:, 3 * CA:])
    padded = jnp.pad(key_value, ((margin, margin), (0, 0)))
    key_index = QBLOCK * jnp.arange(blocks, dtype=jnp.int32)[:, None] + jnp.arange(KWIN, dtype=jnp.int32)[None, :]
    windows = padded[key_index]
    absolute = key_index - margin
    usable = (absolute >= 0) & (absolute < ATOMS)
    query_heads = queries.reshape(blocks, QBLOCK, HEADS, head_dim).astype(jnp.float32)
    key_heads = windows[:, :, :CA].reshape(blocks, KWIN, HEADS, head_dim).astype(jnp.float32)
    value_heads = windows[:, :, CA:].reshape(blocks, KWIN, HEADS, head_dim).astype(jnp.float32)
    scores = jnp.einsum('bqhd,bkhd->bhqk', query_heads, key_heads) / math.sqrt(head_dim) + attn_bias
    scores = jnp.where(usable[:, None, None, :], scores, -1e+30)
    shifted = jnp.exp(scores - lax.optimization_barrier(jnp.max(scores, axis=-1, keepdims=True)))
    weights = (shifted / lax.optimization_barrier(jnp.sum(shifted, axis=-1, keepdims=True))).astype(jnp.bfloat16)
    attended = jnp.einsum('bhqk,bkhd->bqhd', weights.astype(jnp.float32), value_heads).reshape(ATOMS, CA)
    gated = (attended * gating).astype(jnp.bfloat16)
    updated = atoms.astype(jnp.float32) + jnp.dot(gated, w_attn_out, preferred_element_type=jnp.float32)
    hidden = jax.nn.relu(jnp.dot(updated.astype(jnp.bfloat16), w_single, preferred_element_type=jnp.float32)).astype(jnp.bfloat16)
    bounds = jnp.cumsum(token_atoms).astype(jnp.int32)
    owners = jnp.searchsorted(bounds, jnp.arange(ATOMS, dtype=jnp.int32), side='right').astype(jnp.int32)
    token_sums = jax.ops.segment_sum(hidden.astype(jnp.float32), owners, num_segments=TOKENS)
    single = (token_sums / token_atoms.astype(jnp.float32)[:, None]).astype(jnp.bfloat16)
    left_proj = jnp.dot(single, w_pair_left, preferred_element_type=jnp.float32).astype(jnp.bfloat16)
    right_proj = jnp.dot(single, w_pair_right, preferred_element_type=jnp.float32).astype(jnp.bfloat16)
    back_proj = jnp.dot(single, w_atom_back, preferred_element_type=jnp.float32).astype(jnp.bfloat16)
    atoms_out = (updated + back_proj[owners].astype(jnp.float32)).astype(jnp.bfloat16)
    row_block = min(64, TOKENS)
    starts = jnp.arange(TOKENS // row_block, dtype=jnp.int32) * row_block
    tri_in = w_tri_in.astype(jnp.float32)

    def pair_front(first_row):
        pair_rows = lax.dynamic_slice_in_dim(pair, first_row, row_block, 1).astype(jnp.float32)
        left_rows = lax.dynamic_slice_in_dim(left_proj, first_row, row_block, 0).astype(jnp.float32)
        merged = pair_rows + left_rows.T[:, :, None] + right_proj.astype(jnp.float32).T[:, None, :]
        return (merged, layer_norm(merged, 0).astype(jnp.bfloat16))

    def factors(first_row):
        merged, pair_norm = pair_front(first_row)
        inputs = jnp.einsum('cij,cd->dij', pair_norm.astype(jnp.float32), tri_in)
        factor_left = (inputs[:CP] * jax.nn.sigmoid(inputs[CP:2 * CP])).astype(jnp.bfloat16)
        factor_right = (inputs[2 * CP:3 * CP] * jax.nn.sigmoid(inputs[3 * CP:])).astype(jnp.bfloat16)
        return (factor_left, factor_right)
    left_blocks, right_blocks = lax.map(factors, starts)
    factor_left = left_blocks.transpose(1, 0, 2, 3).reshape(CP, TOKENS, TOKENS)
    factor_right = right_blocks.transpose(1, 0, 2, 3).reshape(CP, TOKENS, TOKENS)

    def channel_product(operands):
        return jnp.dot(operands[0], operands[1].T, preferred_element_type=jnp.float32).astype(jnp.bfloat16)
    triangle = lax.map(channel_product, (factor_left, factor_right))

    def finish(first_row):
        merged, pair_norm = pair_front(first_row)
        tri_rows = lax.dynamic_slice_in_dim(triangle, first_row, row_block, 1)
        tri_norm = layer_norm(tri_rows.astype(jnp.float32), 0).astype(jnp.bfloat16)
        update = jnp.einsum('cij,cd->dij', tri_norm.astype(jnp.float32), w_tri_out.astype(jnp.float32))
        gate_pair = jax.nn.sigmoid(jnp.einsum('cij,cd->dij', pair_norm.astype(jnp.float32), w_tri_gate.astype(jnp.float32)))
        return (merged + gate_pair * update).astype(jnp.bfloat16)
    out_blocks = lax.map(finish, starts)
    pair_out = out_blocks.transpose(1, 0, 2, 3).reshape(CP, TOKENS, TOKENS)
    return (atoms_out, pair_out)
```

```python
import functools
import math

import jax
import jax.numpy as jnp
from jax import lax
from jax.experimental import pallas as pl
from jax.experimental.pallas import tpu as pltpu
from jax.sharding import PartitionSpec as P

HEADS = 4
QBLOCK = 32
KWIN = 128
EPSILON = 1e-05
MESH_AXES = ("row", "col")

ROWS_PER_STEP = 32
GROUP = 16
CHUNK = 8
FINISH_CHUNK = 4
FIRST, SECOND = (0, 4), (4, 8)
RIGHT_FIRST, RIGHT_SECOND = (0, 5), (5, 8)
SINGLES = 1280
SLOTS = 8
VMEM_BYTES = 63_000_000
ATOM_VMEM_BYTES = 63_400_000
FRONT_VMEM_BYTES = 62_000_000
TOKEN_VMEM_BYTES = 40_000_000

f32 = jnp.float32
bf16 = jnp.bfloat16


def kernel_params(limit=VMEM_BYTES):
    return pltpu.CompilerParams(vmem_limit_bytes=limit)


def vmem():
    return pl.BlockSpec(memory_space=pltpu.VMEM)


def whole(array):
    return pl.BlockSpec(array.shape, lambda i: (0,) * len(array.shape))


def sigmoid(x):
    return 0.5 * jnp.tanh(0.5 * x) + 0.5


def normalise(values, along):
    average = jnp.mean(values, axis=along, keepdims=True)
    centred = values - average
    variance = jnp.mean(centred * centred, axis=along, keepdims=True)
    return centred * lax.rsqrt(variance + EPSILON)


def dot(a, b, contract_a, contract_b):
    return lax.dot_general(
        a, b, (((contract_a,), (contract_b,)), ((), ())), preferred_element_type=f32
    )


def atom_kernel(
    total_atoms,
    first_ref,
    before_ref,
    after_ref,
    counts_ref,
    *refs,
):
    fetched = refs[:8]
    atoms_out_ref, partial_ref = refs[8:10]
    held, sems = refs[10:18], refs[18]
    copies = [
        pltpu.make_async_copy(source, target, sems.at[k])
        for k, (source, target) in enumerate(zip(fetched, held))
    ]
    for copy in copies:
        copy.start()
    atoms_ref, w_attn_ref, bias_ref, w_attn_out_ref = held[:4]
    w_single_ref, w_back_ref, w_left_ref, w_right_ref = held[4:]
    first = first_ref[0]
    atom_count, width = atoms_ref.shape
    margin = (KWIN - QBLOCK) // 2
    head_dim = width // HEADS
    reach = margin + QBLOCK
    wide = atom_count + 2 * QBLOCK

    counts = counts_ref[...].astype(f32)
    lane_from = lax.broadcasted_iota(jnp.int32, (width, width), 0)
    lane_to = lax.broadcasted_iota(jnp.int32, (width, width), 1)
    earlier = jnp.where(lane_from <= lane_to, 1.0, 0.0).astype(bf16)
    within = dot(counts.astype(bf16), earlier, 1, 0)
    totals = jnp.broadcast_to(within[:, width - 1 :], within.shape)
    so_far = jnp.zeros((1, width), f32)
    ends, begins = [], []
    for row in range(counts.shape[0]):
        row_ends = within[row : row + 1] + so_far
        ends.append(row_ends)
        begins.append(row_ends - counts[row : row + 1])
        so_far = so_far + totals[row : row + 1]
    ends = jnp.concatenate(ends, axis=1).astype(jnp.int32)
    starts = jnp.concatenate(begins, axis=1).astype(jnp.int32)
    tokens = ends.shape[1]
    position = (first - QBLOCK) + lax.broadcasted_iota(jnp.int32, (wide, 1), 0)
    member = jnp.where((starts <= position) & (position < ends), 1.0, 0.0).astype(bf16)
    own_member = member[QBLOCK : QBLOCK + atom_count]
    own_position = position[QBLOCK : QBLOCK + atom_count]
    column = lax.broadcasted_iota(jnp.int32, (1, partial_ref.shape[0] * SLOTS), 1)
    wanted = jnp.where(
        column * 0 + first >= total_atoms - SINGLES,
        first + (column >> (SLOTS.bit_length() - 1)),
        jnp.where(column < tokens - SINGLES, starts[:, : column.shape[1]], -1),
    )
    chosen = jnp.where(wanted == own_position, 1.0, 0.0).astype(bf16)
    together = dot(own_member, member, 1, 1).astype(bf16)
    own_count = jnp.sum(together.astype(f32), axis=1, keepdims=True)

    copies[0].wait()
    atoms = jnp.concatenate(
        [before_ref[:reach], atoms_ref[...].astype(f32), after_ref[:reach]], axis=0
    )
    normed = normalise(atoms, 1).astype(bf16)
    copies[1].wait()
    projected = dot(normed, w_attn_ref[...], 1, 0)
    kv = projected[:, width : 3 * width].astype(bf16)
    queries = projected[margin : margin + wide, :width]
    gating = sigmoid(projected[margin : margin + wide, 3 * width :])
    feature = lax.broadcasted_iota(jnp.int32, (QBLOCK, width), 1)
    in_head = [
        (feature >= head * head_dim) & (feature < (head + 1) * head_dim) for head in range(HEADS)
    ]
    window_at = lax.broadcasted_iota(jnp.int32, (HEADS * QBLOCK, KWIN), 1)
    copies[2].wait()
    attended = []
    blocks = wide // QBLOCK
    for block in range(blocks):
        start = block * QBLOCK
        query = queries[start : start + QBLOCK]
        query_heads = jnp.concatenate(
            [jnp.where(mask, query, 0.0) for mask in in_head], axis=0
        ).astype(bf16)
        keys = kv[start : start + KWIN, :width]
        values = kv[start : start + KWIN, width:]
        if block == 0:
            bias = before_ref[reach:]
        elif block == blocks - 1:
            bias = after_ref[reach:]
        else:
            bias = bias_ref[block - 1]
        scores = dot(query_heads, keys, 1, 1) / math.sqrt(head_dim) + bias
        absolute = window_at + (first + start - reach)
        scores = jnp.where((absolute >= 0) & (absolute < total_atoms), scores, -1e30)
        shifted = jnp.exp(scores - jnp.max(scores, axis=1, keepdims=True))
        weights = (shifted / jnp.sum(shifted, axis=1, keepdims=True)).astype(bf16)
        heads_out = dot(weights, values, 1, 0)
        joined = jnp.zeros((QBLOCK, width), f32)
        for head, mask in enumerate(in_head):
            joined = jnp.where(mask, heads_out[head * QBLOCK : (head + 1) * QBLOCK], joined)
        attended.append(joined)
    gated = (jnp.concatenate(attended, axis=0) * gating).astype(bf16)
    for copy in copies[3:]:
        copy.wait()
    updated = atoms[margin : margin + wide] + dot(gated, w_attn_out_ref[...], 1, 0)
    hidden = jnp.maximum(dot(updated.astype(bf16), w_single_ref[...], 1, 0), 0.0).astype(bf16)
    single = (dot(together, hidden, 1, 0) / own_count).astype(bf16)
    back = dot(single, w_back_ref[...], 1, 0).astype(bf16).astype(f32)
    atoms_out_ref[...] = (updated[QBLOCK : QBLOCK + atom_count] + back).astype(bf16)

    sides = [dot(single, ref[...], 1, 0).astype(bf16) for ref in (w_left_ref, w_right_ref)]
    shape = (partial_ref.shape[0], SLOTS, width)
    partial_ref[...] = jnp.concatenate(
        [dot(chosen, side, 0, 0).reshape(shape) for side in sides], axis=1
    ).astype(bf16)


def spread_kernel(rows, cols, got_ref, out_ref):
    got = got_ref[...].astype(f32)
    devices = rows * cols
    width = got.shape[2]
    first_single = devices - SINGLES // width
    summed = jnp.sum(got[:first_single], axis=0)
    slot = lax.broadcasted_iota(jnp.int32, (SLOTS, width), 0)
    lefts, rights = [], []
    for row in range(rows):
        at = 2 * row - (2 * rows - SINGLES // width)
        if at < 0:
            lefts.append(summed[:SLOTS])
        else:
            at += first_single
            lefts.append(jnp.where(slot == 0, got[at, :SLOTS], got[at + 1, :SLOTS]))
    for col in range(cols):
        at = col - (cols - SINGLES // width)
        rights.append(summed[SLOTS:] if at < 0 else got[first_single + at, SLOTS:])
    for row in range(rows):
        for col in range(cols):
            block = jnp.concatenate([lefts[row], rights[col]], axis=0)
            out_ref[row * cols + col] = block.astype(bf16)


def gather_kernel(rows, cols, place_ref, got_ref, out_ref, held_ref):
    row, col = place_ref[0], place_ref[1]
    devices, slots, width = got_ref.shape
    held_ref[...] = got_ref[...].astype(f32).reshape(devices * slots, width)
    single_rows = rows - SINGLES // width // 2
    single_cols = cols - SINGLES // width
    owners = width // SLOTS

    @pl.when(row < single_rows)
    def _():
        blocks = held_ref[pl.ds(row * (2 * owners * slots), 2 * owners * slots), :]
        out_ref[: 2 * width] = blocks.reshape(2 * owners, slots, width)[:, :SLOTS].reshape(
            2 * width, width
        )

    @pl.when(row >= single_rows)
    def _():
        out_ref[:width] = held_ref[pl.ds(0, width, stride=slots), :]
        out_ref[width : 2 * width] = held_ref[pl.ds(1, width, stride=slots), :]

    @pl.when(col < single_cols)
    def _():
        blocks = held_ref[pl.ds(col * (owners * slots), owners * slots), :]
        right = blocks.reshape(owners, slots, width)[:, SLOTS:].reshape(width, width)
        out_ref[2 * width :] = right.T

    @pl.when(col >= single_cols)
    def _():
        out_ref[2 * width :] = held_ref[pl.ds(SLOTS, width, stride=slots), :].T


def exchange(blocks):
    return lax.all_to_all(blocks, MESH_AXES, split_axis=0, concat_axis=0, tiled=True)


def atom_stage(
    pair,
    atoms,
    token_atoms,
    attn_bias,
    w_attn,
    w_attn_out,
    w_single,
    w_pair_left,
    w_pair_right,
    w_atom_back,
):
    atom_count, width = atoms.shape
    tokens = token_atoms.shape[0]
    rows, cols = lax.axis_size("row"), lax.axis_size("col")
    devices = rows * cols
    reach = (KWIN - QBLOCK) // 2 + QBLOCK
    place = jnp.stack([lax.axis_index("row"), lax.axis_index("col")]).astype(jnp.int32)
    first = (lax.axis_index(MESH_AXES) * atom_count).astype(jnp.int32).reshape(1)
    bias = attn_bias.reshape(atom_count // QBLOCK, HEADS * QBLOCK, KWIN)
    up = [(i, i + 1) for i in range(devices - 1)]
    down = [(j, i) for i, j in up]
    before = lax.ppermute(
        jnp.concatenate([atoms[atom_count - reach :].astype(f32), bias[-1]], axis=0), MESH_AXES, up
    )
    after = lax.ppermute(
        jnp.concatenate([atoms[:reach].astype(f32), bias[0]], axis=0), MESH_AXES, down
    )
    small = (before, after, token_atoms.reshape(tokens // width, width))
    fetched = (
        atoms,
        w_attn,
        bias,
        w_attn_out,
        w_single,
        w_atom_back,
        w_pair_left,
        w_pair_right,
    )
    results = (
        jax.ShapeDtypeStruct((atom_count, width), bf16),
        jax.ShapeDtypeStruct((devices, 2 * SLOTS, width), bf16),
    )
    atoms_out, partial = pl.pallas_call(
        functools.partial(atom_kernel, atom_count * devices),
        out_shape=results,
        grid=(1,),
        in_specs=[pl.BlockSpec(memory_space=pltpu.SMEM)]
        + [whole(x) for x in small]
        + [pl.BlockSpec(memory_space=pltpu.HBM)] * len(fetched),
        out_specs=tuple(whole(x) for x in results),
        scratch_shapes=[pltpu.VMEM(x.shape, x.dtype) for x in fetched]
        + [pltpu.SemaphoreType.DMA((len(fetched),))],
        compiler_params=kernel_params(ATOM_VMEM_BYTES),
        cost_estimate=pl.CostEstimate(
            flops=400_000_000, bytes_accessed=3_000_000, transcendentals=100_000
        ),
        name="atom_attention",
    )(first, *small, *fetched)
    partial, pair = lax.optimization_barrier((partial, pair))
    got = exchange(partial)
    got, lanes = lax.optimization_barrier((got, to_lanes(pair, FIRST, None)))
    spread = pl.pallas_call(
        functools.partial(spread_kernel, rows, cols),
        out_shape=jax.ShapeDtypeStruct(got.shape, bf16),
        in_specs=[vmem()],
        out_specs=vmem(),
        compiler_params=kernel_params(TOKEN_VMEM_BYTES),
        name="spread_tokens",
    )(got)
    spread, pair = lax.optimization_barrier((spread, pair))
    shared = exchange(spread)
    shared, lanes = lax.optimization_barrier((shared, to_lanes(pair, SECOND, lanes)))
    sides = pl.pallas_call(
        functools.partial(gather_kernel, rows, cols),
        out_shape=jax.ShapeDtypeStruct((3 * width, width), f32),
        in_specs=[pl.BlockSpec(memory_space=pltpu.SMEM), vmem()],
        out_specs=vmem(),
        scratch_shapes=[pltpu.VMEM((devices * 2 * SLOTS, width), f32)],
        compiler_params=kernel_params(TOKEN_VMEM_BYTES),
        name="gather_tokens",
    )(place, shared)
    return atoms_out, lanes, sides


def interleave(*weights):
    channels = weights[0].shape[0]
    tiles = jnp.stack([w.reshape(channels // 8, 8, w.shape[1]) for w in weights], axis=1)
    return tiles.reshape(len(weights) * channels, weights[0].shape[1])


def turned_scratch(channels):
    return pltpu.VMEM((ROWS_PER_STEP // GROUP, channels * GROUP, 128), f32)


def lanes_kernel(pair_ref, *rest):
    out_ref, turned_ref = rest[-2:]
    channels = pair_ref.shape[0]
    for group in range(ROWS_PER_STEP // GROUP):
        rows = slice(group * GROUP, (group + 1) * GROUP)
        turned_ref[group] = pair_ref[:, rows, :].astype(f32).reshape(channels * GROUP, 128)
        for i in range(GROUP):
            at = (group * GROUP + i) * 128
            out_ref[:, at : at + 128] = turned_ref[
                group, pl.ds(i, channels, stride=GROUP), :
            ].astype(bf16)


def right_spec(sides):
    width = sides.shape[1]
    return pl.BlockSpec((width, width), lambda i: (sides.shape[0] // width - 1, 0))


def written_into(operands, in_specs, so_far):
    if so_far is None:
        return operands, in_specs, {}
    spec = pl.BlockSpec(memory_space=pltpu.HBM)
    return operands + (so_far,), in_specs + [spec], {len(operands): 0}


def to_lanes(pair, part, so_far):
    channels, tile_rows, _ = pair.shape
    first, steps = part[0], part[1] - part[0]
    step_lanes = ROWS_PER_STEP * 128
    operands, in_specs, aliases = written_into(
        (pair,),
        [pl.BlockSpec((channels, ROWS_PER_STEP, 128), lambda i: (0, first + i, 0))],
        so_far,
    )
    return pl.pallas_call(
        lanes_kernel,
        grid=(steps,),
        out_shape=jax.ShapeDtypeStruct((channels, tile_rows * 128), bf16),
        in_specs=in_specs,
        out_specs=pl.BlockSpec((channels, step_lanes), lambda i: (0, first + i)),
        input_output_aliases=aliases,
        scratch_shapes=[turned_scratch(channels)],
        compiler_params=kernel_params(),
        cost_estimate=pl.CostEstimate(
            flops=0, bytes_accessed=4 * channels * steps * step_lanes, transcendentals=0
        ),
        name=f"pair_lanes_{first}",
    )(*operands)


def projections_of(left, right, row, chunk):
    return jnp.concatenate(
        [jnp.broadcast_to(left[:, row + i : row + i + 1], right.shape) + right for i in range(chunk)],
        axis=1,
    )


def store_turned(turned_ref, group, row, values):
    channels = values.shape[0]
    for i in range(values.shape[1] // 128):
        turned_ref[group, pl.ds(row + i, channels, stride=GROUP), :] = values[
            :, i * 128 : (i + 1) * 128
        ]


def each_chunk(chunk, prepare, use):
    places = []
    for group in range(ROWS_PER_STEP // GROUP):
        for row in range(0, GROUP, chunk):
            start = (group * GROUP + row) * 128
            places.append((group, row, slice(start, start + chunk * 128)))
    ready = prepare(*places[0])
    for n, place in enumerate(places):
        following = prepare(*places[n + 1]) if n + 1 < len(places) else None
        use(*place, ready)
        ready = following


def front_kernel(parts, pair_ref, left_ref, right_ref, w_ref, *rest):
    gate_refs = rest[-2:-1] if parts % 2 else ()
    out_ref, turned_ref = rest[-2 - parts % 2], rest[-1]
    channels = pair_ref.shape[0]
    weights = w_ref[...]
    left = left_ref[...].T

    def prepare(group, row, at):
        merged = pair_ref[:, at].astype(f32) + projections_of(
            left, right_ref[...], group * GROUP + row, CHUNK
        )
        return dot(weights, normalise(merged, 0).astype(bf16), 1, 0)

    def use(group, row, at, inputs):
        inputs = inputs.reshape(channels // 8, parts, 8, CHUNK * 128)
        factor = inputs[:, 0] * jnp.tanh(inputs[:, 1]) + inputs[:, 0]
        store_turned(turned_ref, group, row, factor.reshape(channels, CHUNK * 128))
        if gate_refs:
            gate = 0.5 * jnp.tanh(inputs[:, parts - 1]) + 0.5
            gate_refs[0][:, at] = gate.reshape(channels, CHUNK * 128).astype(bf16)
        if row + CHUNK == GROUP:
            rows = slice(group * GROUP, (group + 1) * GROUP)
            out_ref[:, rows, :] = turned_ref[group].reshape(channels, GROUP, 128).astype(bf16)

    each_chunk(CHUNK, prepare, use)


def front(pair_lanes, sides, weights, part, name, place=0, total=None, so_far=None):
    channels = pair_lanes.shape[0]
    parts = weights.shape[0] // channels
    first, steps = part[0], part[1] - part[0]
    total = total or steps
    step_lanes = ROWS_PER_STEP * 128
    out_shape = [jax.ShapeDtypeStruct((channels, total * ROWS_PER_STEP, 128), bf16)]
    out_specs = [pl.BlockSpec((channels, ROWS_PER_STEP, 128), lambda i: (0, place + i, 0))]
    if parts % 2:
        out_shape.append(jax.ShapeDtypeStruct((channels, steps * step_lanes), bf16))
        out_specs.append(pl.BlockSpec((channels, step_lanes), lambda i: (0, i)))
    elements = channels * steps * step_lanes
    operands, in_specs, aliases = written_into(
        (pair_lanes, sides, sides, weights),
        [
            pl.BlockSpec((channels, step_lanes), lambda i: (0, first + i)),
            pl.BlockSpec((ROWS_PER_STEP, channels), lambda i: (first + i, 0)),
            right_spec(sides),
            pl.BlockSpec(weights.shape, lambda i: (0, 0)),
        ],
        so_far,
    )
    return pl.pallas_call(
        functools.partial(front_kernel, parts),
        grid=(steps,),
        out_shape=out_shape,
        in_specs=in_specs,
        out_specs=out_specs,
        input_output_aliases=aliases,
        scratch_shapes=[turned_scratch(channels)],
        compiler_params=kernel_params(FRONT_VMEM_BYTES),
        cost_estimate=pl.CostEstimate(
            flops=2 * elements * weights.shape[0],
            bytes_accessed=2 * elements * parts,
            transcendentals=elements * (parts - 1),
        ),
        name=name,
    )(*operands)


def triangle_kernel(left_at, right_at, left_ref, *refs):
    right_refs, out_ref = refs[:-1], refs[-1]
    rows, cols = left_ref.shape[:2]
    right = jnp.concatenate(
        [
            jnp.concatenate([ref[q, at] for q in range(cols)], axis=1)
            for ref, at in zip(right_refs, right_at)
        ],
        axis=0,
    )
    left = jnp.concatenate(
        [
            jnp.concatenate([left_ref[r, q, left_at] for q in range(cols)], axis=1)
            for r in range(rows)
        ],
        axis=0,
    )
    product = dot(left, right, 1, 1).astype(bf16)
    part_rows = out_ref.shape[2]
    for r in range(rows):
        block = product[r * part_rows : (r + 1) * part_rows]
        out_ref[r, 0] = block[:, :128]
        out_ref[r, 1] = block[:, 128:]


def triangle(left, left_at, rights, right_at, rows, cols, name):
    devices, held_rows, _ = left.shape
    part_rows = left_at.stop - left_at.start
    tokens = cols * 128
    left_grid = left.reshape(rows, cols, held_rows, 128)
    product = pl.pallas_call(
        functools.partial(triangle_kernel, left_at, right_at),
        grid=(rows,),
        out_shape=jax.ShapeDtypeStruct((rows, cols, part_rows, 128), bf16),
        in_specs=[
            pl.BlockSpec(left_grid.shape, lambda r: (0, 0, 0, 0), pipeline_mode=pl.Buffered(1)),
        ]
        + [pl.BlockSpec((cols,) + right.shape[1:], lambda r: (r, 0, 0)) for right in rights],
        out_specs=pl.BlockSpec((rows, cols // rows, part_rows, 128), lambda r: (0, r, 0, 0)),
        compiler_params=kernel_params(),
        cost_estimate=pl.CostEstimate(
            flops=2 * rows * part_rows * tokens * tokens,
            bytes_accessed=2 * tokens * (2 * rows * part_rows + tokens),
            transcendentals=0,
        ),
        name=name,
    )(left_grid, *rights)
    return product.reshape(devices, part_rows, 128)


def finish_kernel(back_ref, gate_ref, pair_ref, left_ref, right_ref, w_ref, *rest):
    out_ref, turned_ref, change_ref = rest[-3:]
    channels = pair_ref.shape[0]
    weights = w_ref[...]
    left = left_ref[...].T

    def prepare(group, row, at):
        if row == 0:
            turned_ref[group] = (
                back_ref[:, group * GROUP : (group + 1) * GROUP, :]
                .astype(f32)
                .reshape(channels * GROUP, 128)
            )
        products = jnp.concatenate(
            [
                turned_ref[group, pl.ds(row + i, channels, stride=GROUP), :]
                for i in range(FINISH_CHUNK)
            ],
            axis=1,
        )
        return dot(weights, normalise(products, 0).astype(bf16), 1, 0)

    def use(group, row, at, update):
        change = (
            projections_of(left, right_ref[...], group * GROUP + row, FINISH_CHUNK)
            + gate_ref[:, at].astype(f32) * update
        )
        store_turned(change_ref, group, row, change)
        if row + FINISH_CHUNK == GROUP:
            rows = slice(group * GROUP, (group + 1) * GROUP)
            out_ref[:, rows, :] = (
                pair_ref[:, rows, :].astype(f32)
                + change_ref[group].reshape(channels, GROUP, 128)
            ).astype(bf16)

    each_chunk(FINISH_CHUNK, prepare, use)


def finish(back, gate, pair, sides, weights, part, so_far):
    channels, tile_rows, _ = pair.shape
    step_lanes = ROWS_PER_STEP * 128
    first, steps = part[0], part[1] - part[0]
    block = pl.BlockSpec((channels, ROWS_PER_STEP, 128), lambda i: (0, first + i, 0))
    operands, in_specs, aliases = written_into(
        (back, gate, pair, sides, sides, weights),
        [
            pl.BlockSpec((channels, ROWS_PER_STEP, 128), lambda i: (0, i, 0)),
            pl.BlockSpec((channels, step_lanes), lambda i: (0, i)),
            block,
            pl.BlockSpec((ROWS_PER_STEP, channels), lambda i: (first + i, 0)),
            right_spec(sides),
            pl.BlockSpec(weights.shape, lambda i: (0, 0)),
        ],
        so_far,
    )
    return pl.pallas_call(
        finish_kernel,
        grid=(steps,),
        out_shape=jax.ShapeDtypeStruct(pair.shape, bf16),
        in_specs=in_specs,
        out_specs=block,
        input_output_aliases=aliases,
        scratch_shapes=[turned_scratch(channels)] * 2,
        compiler_params=kernel_params(),
        cost_estimate=pl.CostEstimate(
            flops=2 * back.size * channels, bytes_accessed=8 * back.size, transcendentals=0
        ),
        name=f"pair_finish_{first}",
    )(*operands)


def on_device(
    atoms,
    pair,
    token_atoms,
    attn_bias,
    w_attn,
    w_attn_out,
    w_single,
    w_pair_left,
    w_pair_right,
    w_atom_back,
    w_tri_in,
    w_tri_gate,
    w_tri_out,
):
    rows, cols = lax.axis_size("row"), lax.axis_size("col")
    channels, tile_rows, tile_cols = pair.shape
    atoms_out, lanes, sides = atom_stage(
        pair,
        atoms,
        token_atoms,
        attn_bias,
        w_attn,
        w_attn_out,
        w_single,
        w_pair_left,
        w_pair_right,
        w_atom_back,
    )
    tri_in = 0.5 * w_tri_in.T.reshape(4, channels, channels)
    right_weights = interleave(tri_in[2], tri_in[3])
    left_weights = interleave(tri_in[0], tri_in[1], 0.5 * w_tri_gate.T)
    hold = lax.optimization_barrier

    (right_a,) = front(lanes, sides, right_weights, RIGHT_FIRST, "right_first")
    right_a, lanes = hold((right_a, lanes))
    got_a = exchange(right_a)
    rights_b = RIGHT_SECOND[1] - RIGHT_SECOND[0]
    steps_b = rights_b + SECOND[1] - SECOND[0]
    (both_b,) = front(lanes, sides, right_weights, RIGHT_SECOND, "right_second", 0, steps_b)
    both_b, gate_1 = front(
        lanes, sides, left_weights, SECOND, "left_second", rights_b, steps_b, both_b
    )
    both_b, lanes, got_a = hold((both_b, lanes, got_a))
    got_b = exchange(both_b)
    left_0, gate_0 = front(lanes, sides, left_weights, FIRST, "left_first")
    left_0, got_b = hold((left_0, got_b))
    got_left_0 = exchange(left_0)
    rights = (got_a, got_b)
    right_at = (slice(0, got_a.shape[1]), slice(0, rights_b * ROWS_PER_STEP))
    left_at = slice(rights_b * ROWS_PER_STEP, steps_b * ROWS_PER_STEP)
    products_1 = triangle(got_b, left_at, rights, right_at, rows, cols, "triangle_second")
    products_1, got_left_0 = hold((products_1, got_left_0))
    back_1 = exchange(products_1)
    left_at = slice(0, got_left_0.shape[1])
    products_0 = triangle(got_left_0, left_at, rights, right_at, rows, cols, "triangle_first")
    products_0, back_1 = hold((products_0, back_1))
    back_0 = exchange(products_0)
    out_weights = w_tri_out.T
    pair_out = finish(back_1, gate_1, pair, sides, out_weights, SECOND, None)
    pair_out = finish(back_0, gate_0, pair, sides, out_weights, FIRST, pair_out)
    return (atoms_out, pair_out)


def solution(mesh):
    in_specs = (
        P(("row", "col"), None),
        P(None, "row", "col"),
        P(),
        P(("row", "col"), None, None, None),
        P(),
        P(),
        P(),
        P(),
        P(),
        P(),
        P(),
        P(),
        P(),
    )
    out_specs = (P(("row", "col"), None), P(None, "row", "col"))
    return jax.shard_map(
        on_device, mesh=mesh, in_specs=in_specs, out_specs=out_specs, check_vma=False
    )
```
